128 devices in a mesh: gx: 8 (over y, z_hi), gy: 4 (over x), gz: 4 (over z_lo, core).
Axes of the slice: x: 4, y: 4, z: 4 (z_hi: 2, z_lo: 2; z = z_hi * 2 + z_lo), core: 2. Of those that a mesh axis runs over, the one named last changes fastest.
Arguments:
- field_window: float32 [16, 32, 1024, 1024], P('gx', None, 'gy', 'gz'), may hold values from -54 to 54
- second_factor: float32 [1024, 64], P('gy'), may hold values from -1 to 1
- third_factor: float32 [1024, 64], P('gz'), may hold values from -1 to 1
- species_factor: float32 [32, 8], replicated, may hold values from -3 to 3
Outputs:
- core_tensor: float32 [64, 64, 16, 8], P('gy', 'gz', 'gx')
- mode_gram: float32 [16, 16], P('gx')
The draws below stay inside these ranges and needn't reach their ends.
All inputs are finite; a program needn't handle non-finite values.
Results may differ from the reference program's by a relative error of at most 0.00007.
Values sent between devices are 32-bit elements; how exact they have to be, the bound alone decides.
No kernel may reach another device: no remote copies, remote signals or barrier semaphores. Data moves between devices by JAX's collectives and lax.ppermute only.
A program may use at most 64 MiB of HBM per device.

```python
import math
import jax
import jax.numpy as jnp
from jax import lax

SPECIES = 32
RANK_S = 8
RANK_Y = 64
RANK_Z = 64
NX = 16
NY = 1024
NZ = 1024


def plane_scales(key, columns_count, lower, upper):
    return jnp.exp(jax.random.uniform(key, (columns_count, 1, 1, 1), jnp.float32, math.log(lower), math.log(upper)))


def column_scales(key, columns_count, spread):
    positions = jnp.arange(columns_count, dtype=jnp.float32) / max(columns_count - 1, 1)
    jitter = jax.random.uniform(key, (1, columns_count), jnp.float32, -0.3, 0.3)
    return jnp.exp(positions * math.log(spread))[None, :] * jnp.exp(jitter)


def draw_field_window(key, part):
    key = jax.random.fold_in(key, 11)
    subkeys = jax.random.split(key, 4)
    noise_part = jnp.clip(jax.random.normal(subkeys[0], (NX, SPECIES, NY, NZ), jnp.float32), -4.0, 4.0)
    shared = jnp.clip(jax.random.normal(subkeys[1], (1, SPECIES, NY, NZ), jnp.float32), -4.0, 4.0)
    mixing = 0.5
    planes = plane_scales(subkeys[2], NX, 0.35, 3.0)
    species_scales = jnp.exp(jax.random.uniform(subkeys[3], (1, SPECIES, 1, 1), jnp.float32, math.log(0.3), math.log(3.0)))
    return planes * species_scales * (noise_part + mixing * shared)


def draw_second_factor(key, part):
    key = jax.random.fold_in(key, 23)
    subkeys = jax.random.split(key, 2)
    entries = jnp.clip(jax.random.normal(subkeys[0], (NY, RANK_Y), jnp.float32), -4.0, 4.0)
    return entries * column_scales(subkeys[1], RANK_Y, 1.8) / math.sqrt(NY)


def draw_third_factor(key, part):
    key = jax.random.fold_in(key, 37)
    subkeys = jax.random.split(key, 2)
    entries = jnp.clip(jax.random.normal(subkeys[0], (NZ, RANK_Z), jnp.float32), -4.0, 4.0)
    return entries * column_scales(subkeys[1], RANK_Z, 1.8) / math.sqrt(NZ)


def draw_species_factor(key, part):
    key = jax.random.fold_in(key, 41)
    subkeys = jax.random.split(key, 2)
    entries = jnp.clip(jax.random.normal(subkeys[0], (SPECIES, RANK_S), jnp.float32), -4.0, 4.0)
    return entries * column_scales(subkeys[1], RANK_S, 1.8) / math.sqrt(SPECIES)


def setup_inputs(seed: int = 0) -> dict:
    splits = jax.random.split(jax.random.key(seed), 5)
    return {
        "field_window": draw_field_window(jax.random.fold_in(splits[4], 71), 0),
        "second_factor": draw_second_factor(jax.random.fold_in(splits[4], 71), 0),
        "third_factor": draw_third_factor(jax.random.fold_in(splits[4], 71), 0),
        "species_factor": draw_species_factor(jax.random.fold_in(splits[4], 71), 0),
    }


HIGHEST = lax.Precision.HIGHEST


def project_plane(window_plane, second_factor, third_factor, species_factor):
    reduced = jnp.einsum("syz,sr->ryz", window_plane, species_factor, precision=HIGHEST)
    along_second = jnp.einsum("ryz,ya->raz", reduced, second_factor, precision=HIGHEST)
    return jnp.einsum("raz,zb->abr", along_second, third_factor, precision=HIGHEST)


def reference(field_window, second_factor, third_factor, species_factor):
    def one_plane(window_plane):
        return project_plane(window_plane, second_factor, third_factor, species_factor)

    stacked = lax.map(one_plane, field_window)
    core_tensor = jnp.transpose(stacked, (1, 2, 0, 3))
    summed = jnp.einsum("pabr,qabr->pq", stacked, stacked, precision=HIGHEST)
    mode_gram = summed / jnp.float32(RANK_S * RANK_Y * RANK_Z)
    return core_tensor, mode_gram
```

```python
import jax
import jax.numpy as jnp
from jax import lax
from jax.experimental import pallas as pl
from jax.experimental.pallas import tpu as pltpu
from jax.sharding import PartitionSpec as P

HIGHEST = lax.Precision.HIGHEST
F32 = jnp.float32
BF16 = jnp.bfloat16
AXES = ("gx", "gy", "gz")
ROWS = 32


def split(v):
    high = v.astype(BF16)
    return high, (v - high.astype(F32)).astype(BF16)


def dot(a, b):
    return jnp.dot(a, b, preferred_element_type=F32)


def mask(shape, f):
    i = lax.broadcasted_iota(jnp.int32, shape, 0)
    j = lax.broadcasted_iota(jnp.int32, shape, 1)
    return jnp.where(f(i, j), 1.0, 0.0).astype(F32)


def project_kernel(field, second, third, species, out, window, spread, high, low, sems):
    planes, count, rows, columns = field.shape
    per = rows // ROWS

    def copy(c):
        p, k = c // per, c % per
        return pltpu.make_async_copy(
            field.at[p, :, pl.ds(k * ROWS, ROWS), :], window.at[c], sems.at[c]
        )

    for c in range(planes * per):
        copy(c).start()
    x = lax.axis_index("gy")
    z = lax.axis_index("gz") // 2

    r_of = mask((64, 8), lambda i, j: i // 8 == j)
    s_of = mask((32, 256), lambda i, j: j // 8 == i)
    w = jnp.dot(jnp.dot(r_of, species[...], precision=HIGHEST), s_of, precision=HIGHEST)
    w_high, w_low = split(w * mask((64, 256), lambda i, j: i % 8 == j % 8))
    spread[0:64] = w_high
    spread[64:128] = w_low

    def rank_second(i):
        first = jnp.where(i // 32 == 0, x, 3 - x)
        return jnp.where(i // 16 % 2 == 0, first, first ^ 1) * 16 + i % 16

    u = jnp.dot(mask((64, 64), lambda i, j: rank_second(i) == j), second[...], precision=HIGHEST)
    u_high, u_low = split(u)
    u_both = jnp.concatenate([u_high, u_low], axis=0)

    pick = mask((256, 64), lambda i, j: j == jnp.where(i // 128 == 0, z, 1 - z) * 32 + i % 32)
    v = lax.dot_general(third[...], pick, (((0,), (1,)), ((), ())), precision=HIGHEST)
    v_high, v_low = split(v)
    lane = lax.broadcasted_iota(jnp.int32, (64, 256), 1) % 128 // 32

    for p in range(planes):

        def step(k, carry, p=p):
            c = p * per + k
            copy(c).wait()
            w_both = spread[...]
            for g in range(ROWS // 16):
                parts = []
                for h in range(2):
                    f = window[c, :, g * 16 + h * 8 : g * 16 + h * 8 + 8, :]
                    f_high, f_low = split(f.reshape(count * 8, columns))
                    d = dot(w_both, f_high)
                    d = d[:64] + d[64:] + dot(w_both[:64], f_low)
                    parts.append(d.reshape(8, 8, columns))
                r_high, r_low = split(jnp.concatenate(parts, axis=1))
                at = pl.ds(pl.multiple_of(k * ROWS + g * 16, 16), 16)
                high[:, at, :] = r_high
                low[:, at, :] = r_low
            return carry

        lax.fori_loop(0, per, step, 0)
        for half in range(2):
            total = jnp.zeros((64, 256), F32)
            for q in range(4):
                r = half * 4 + q
                d = dot(u_both, high[r])
                t_high, t_low = split(d[:64] + d[64:] + dot(u_high, low[r]))
                e = dot(jnp.concatenate([t_high, t_low], axis=0), v_high)
                total = jnp.where(lane == q, e[:64] + e[64:] + dot(t_high, v_low), total)
            for zs in range(2):
                for xs in range(4):
                    at = zs * 256 + xs * 64 + p * 32 + half * 16
                    out[at : at + 16, :] = total[xs * 16 : xs * 16 + 16, zs * 128 : zs * 128 + 128]


def project(field, second, third, species):
    planes, count, rows, columns = field.shape
    vmem = pl.BlockSpec(memory_space=pltpu.VMEM)
    pieces = planes * rows // ROWS
    return pl.pallas_call(
        project_kernel,
        out_shape=jax.ShapeDtypeStruct((512, 128), F32),
        in_specs=[pl.BlockSpec(memory_space=pl.ANY), vmem, vmem, vmem],
        out_specs=vmem,
        scratch_shapes=[
            pltpu.VMEM((pieces, count, ROWS, columns), F32),
            pltpu.VMEM((128, 256), BF16),
            pltpu.VMEM((8, rows, columns), BF16),
            pltpu.VMEM((8, rows, columns), BF16),
            pltpu.SemaphoreType.DMA((pieces,)),
        ],
        compiler_params=pltpu.CompilerParams(vmem_limit_bytes=48 << 20),
        cost_estimate=pl.CostEstimate(
            flops=1 << 32, bytes_accessed=17 << 20, transcendentals=0
        ),
    )(field, second, third, species)


def gram_kernel(near, far, out):
    gx = lax.axis_index("gx")
    y, h = gx // 2, gx % 2
    ones = jnp.ones((128, 128), F32)
    plane = lax.broadcasted_iota(jnp.int32, (16, 128), 0)
    lane = lax.broadcasted_iota(jnp.int32, (16, 128), 1)
    block = plane // 2
    first = jnp.where(block // 4 == 0, y, 3 - y)
    owner = jnp.where(block // 2 % 2 == 0, first, first ^ 1) * 2 + (h ^ (block % 2))
    here = lane == owner * 2 + plane % 2
    rows = []
    for p in range(2):
        mine = near[p * 32 : p * 32 + 32, :]
        terms = []
        for ref in (near, far):
            for m in range(8):
                terms.append(jnp.sum(mine * ref[m * 32 : m * 32 + 32, :], axis=0, keepdims=True))
        sums = jnp.sum(jnp.concatenate(terms, axis=0), axis=1, keepdims=True)
        rows.append(jnp.sum(jnp.where(here, sums, 0.0), axis=0, keepdims=True))
    rows.append(jnp.zeros((6, 128), F32))
    out[...] = jnp.concatenate(rows, axis=0) * (1.0 / 32768.0)


def gram(near, far):
    vmem = pl.BlockSpec(memory_space=pltpu.VMEM)
    return pl.pallas_call(
        gram_kernel,
        out_shape=jax.ShapeDtypeStruct((8, 128), F32),
        in_specs=[vmem, vmem],
        out_specs=vmem,
        cost_estimate=pl.CostEstimate(flops=1 << 20, bytes_accessed=1 << 18, transcendentals=0),
    )(near, far)


def arrange_kernel(one, other, out):
    core = lax.axis_index("gz") % 2
    block = jnp.where(core == 1, one[...], other[...])
    block = jnp.where(core == 1, pltpu.roll(block, 112, 1), block)
    for p in range(2):
        for half in range(2):
            at = p * 32 + half * 16
            for q in range(4):
                out[:, p, half * 4 + q, :] = block[at : at + 16, q * 32 : q * 32 + 16]


def arrange(one, other):
    vmem = pl.BlockSpec(memory_space=pltpu.VMEM)
    return pl.pallas_call(
        arrange_kernel,
        out_shape=jax.ShapeDtypeStruct((16, 2, 8, 16), F32),
        in_specs=[vmem, vmem],
        out_specs=vmem,
        cost_estimate=pl.CostEstimate(flops=1 << 16, bytes_accessed=1 << 18, transcendentals=0),
    )(one, other)


CHIPS = [(y, h, x, z) for y in range(4) for h in range(2) for x in range(4) for z in range(2)]


def index(y, h, x, z, core):
    return (y * 2 + h) * 16 + x * 4 + z * 2 + core


def swap(v):
    pairs = [(index(*chip, c), index(*chip, 1 - c)) for chip in CHIPS for c in range(2)]
    return lax.ppermute(v, AXES, pairs)


def send(v, core, to):
    pairs = []
    for chip in CHIPS:
        pairs.append((index(*chip, core), index(*to(*chip), 1 - core)))
        pairs.append((index(*chip, 1 - core), index(*chip, core)))
    return lax.ppermute(v, AXES, pairs)


def over_z(y, h, x, z):
    return y, h, x, 1 - z


def over_x(y, h, x, z):
    return y, h, x ^ 1, z


def across_x(y, h, x, z):
    return y, h, 3 - x, z


def over_h(y, h, x, z):
    return y, 1 - h, x, z


def over_y(y, h, x, z):
    return y ^ 1, h, x, z


def across_y(y, h, x, z):
    return 3 - y, h, x, z


def on_device(field_window, second_factor, third_factor, species_factor):
    part = project(field_window, second_factor.T, third_factor.T, species_factor.T)
    with jax.named_scope("reduce"):
        part = part + swap(part)
        core = 0
        for to in (over_z, across_x, over_x):
            keep = part.shape[0] // 2
            mine = swap(part[:keep])
            part = mine + send(part[keep:], core, to)
            core = 1 - core
    with jax.named_scope("gather"):
        near = part
        for to in (over_h, over_y, across_y):
            mine = swap(near)
            far = send(near, core, to)
            if to is over_h:
                other = mine
            if to is not across_y:
                near = jnp.concatenate([mine, far])
            core = 1 - core
    core_tensor = jnp.transpose(arrange(part, other), (0, 3, 1, 2))
    with jax.named_scope("gram"):
        total = gram(mine, far)
        for to in (over_x, across_x, over_z):
            mine = swap(total)
            total = mine + send(total, core, to)
            core = 1 - core
        mine = swap(total)
        mode_gram = jnp.where(lax.axis_index("gz") % 2 == core, total, mine)[:2, :16]
    return (core_tensor, mode_gram)


def solution(mesh):
    in_specs = (P("gx", None, "gy", "gz"), P("gy", None), P("gz", None), P())
    out_specs = (P("gy", "gz", "gx", None), P("gx", None))
    return jax.shard_map(
        on_device, mesh=mesh, in_specs=in_specs, out_specs=out_specs, check_vma=False
    )
```

```python
import jax
import jax.numpy as jnp
from jax import lax
from jax.experimental import pallas as pl
from jax.experimental.pallas import tpu as pltpu
from jax.sharding import PartitionSpec as P

HIGHEST = lax.Precision.HIGHEST
F32 = jnp.float32
BF16 = jnp.bfloat16
AXES = ("gx", "gy", "gz")
ROWS = 32


def split(v):
    high = v.astype(BF16)
    return high, (v - high.astype(F32)).astype(BF16)


def dot(a, b):
    return jnp.dot(a, b, preferred_element_type=F32)


def mask(shape, f):
    i = lax.broadcasted_iota(jnp.int32, shape, 0)
    j = lax.broadcasted_iota(jnp.int32, shape, 1)
    return jnp.where(f(i, j), 1.0, 0.0).astype(F32)


def project_kernel(
    field, second_hbm, third_hbm, species_hbm, out, window, spread, high, low,
    second, third, species, sems, factor_sems,
):
    planes, count, rows, columns = field.shape
    per = rows // ROWS

    def copy(c):
        p, k = c // per, c % per
        return pltpu.make_async_copy(
            field.at[p, :, pl.ds(k * ROWS, ROWS), :], window.at[c], sems.at[c]
        )

    factors = [
        pltpu.make_async_copy(source, target, factor_sems.at[i])
        for i, (source, target) in enumerate(
            ((species_hbm, species), (second_hbm, second), (third_hbm, third))
        )
    ]
    for factor in factors:
        factor.start()
    for c in range(2):
        copy(c).start()
    for factor in factors:
        factor.wait()
    for c in range(2, planes * per):
        copy(c).start()
    x = lax.axis_index("gy")
    z = lax.axis_index("gz") // 2

    r_of = mask((64, 8), lambda i, j: i // 8 == j)
    s_of = mask((32, 256), lambda i, j: j // 8 == i)
    w = jnp.dot(jnp.dot(r_of, species[...], precision=HIGHEST), s_of, precision=HIGHEST)
    w_high, w_low = split(w * mask((64, 256), lambda i, j: i % 8 == j % 8))
    spread[0:64] = w_high
    spread[64:128] = w_low

    def rank_second(i):
        return (x + i // 16) % 4 * 16 + i % 16

    u = jnp.dot(mask((64, 64), lambda i, j: rank_second(i) == j), second[...], precision=HIGHEST)
    u_high, u_low = split(u)
    u_both = jnp.concatenate([u_high, u_low], axis=0)

    pick = mask((256, 64), lambda i, j: j == jnp.where(i // 128 == 0, z, 1 - z) * 32 + i % 32)
    v = lax.dot_general(third[...], pick, (((0,), (1,)), ((), ())), precision=HIGHEST)
    v_high, v_low = split(v)
    lane = lax.broadcasted_iota(jnp.int32, (64, 256), 1) % 128 // 32

    for p in range(planes):

        def step(k, carry, p=p):
            c = p * per + k
            copy(c).wait()
            w_both = spread[...]
            for g in range(ROWS // 16):
                parts = []
                for h in range(2):
                    f = window[c, :, g * 16 + h * 8 : g * 16 + h * 8 + 8, :]
                    f_high, f_low = split(f.reshape(count * 8, columns))
                    d = dot(w_both, f_high)
                    d = d[:64] + d[64:] + dot(w_both[:64], f_low)
                    parts.append(d.reshape(8, 8, columns))
                r_high, r_low = split(jnp.concatenate(parts, axis=1))
                at = pl.ds(pl.multiple_of(k * ROWS + g * 16, 16), 16)
                high[:, at, :] = r_high
                low[:, at, :] = r_low
            return carry

        lax.fori_loop(0, per, step, 0)
        for half in range(2):
            total = jnp.zeros((64, 256), F32)
            for q in range(4):
                r = half * 4 + q
                d = dot(u_both, high[r])
                t_high, t_low = split(d[:64] + d[64:] + dot(u_high, low[r]))
                e = dot(jnp.concatenate([t_high, t_low], axis=0), v_high)
                total = jnp.where(lane == q, e[:64] + e[64:] + dot(t_high, v_low), total)
            for zs in range(2):
                for xs in range(4):
                    at = zs * 256 + xs * 64 + p * 32 + half * 16
                    out[at : at + 16, :] = total[xs * 16 : xs * 16 + 16, zs * 128 : zs * 128 + 128]


def project(field, second, third, species):
    planes, count, rows, columns = field.shape
    vmem = pl.BlockSpec(memory_space=pltpu.VMEM)
    pieces = planes * rows // ROWS
    return pl.pallas_call(
        project_kernel,
        out_shape=jax.ShapeDtypeStruct((512, 128), F32),
        in_specs=[pl.BlockSpec(memory_space=pltpu.HBM)] * 4,
        out_specs=vmem,
        scratch_shapes=[
            pltpu.VMEM((pieces, count, ROWS, columns), F32),
            pltpu.VMEM((128, 256), BF16),
            pltpu.VMEM((8, rows, columns), BF16),
            pltpu.VMEM((8, rows, columns), BF16),
            pltpu.VMEM(second.shape, F32),
            pltpu.VMEM(third.shape, F32),
            pltpu.VMEM(species.shape, F32),
            pltpu.SemaphoreType.DMA((pieces,)),
            pltpu.SemaphoreType.DMA((3,)),
        ],
        compiler_params=pltpu.CompilerParams(vmem_limit_bytes=60 << 20),
        cost_estimate=pl.CostEstimate(
            flops=1 << 32, bytes_accessed=17 << 20, transcendentals=0
        ),
    )(field, second, third, species)


def gram_kernel(two, one, three, mine, out):
    gx = lax.axis_index("gx")
    y, h = gx // 2, gx % 2
    sums = []
    for p in range(2):
        own = mine[64 + p * 32 : 96 + p * 32, :]
        for ref in (mine, one, two, three):
            for m in range(4):
                product = own * ref[m * 32 : m * 32 + 32, :]
                sums.append(product[0:8] + product[8:16] + product[16:24] + product[24:32])
    sums = jnp.sum(jnp.concatenate(sums, axis=0), axis=1, keepdims=True)
    row = lax.broadcasted_iota(jnp.int32, (256, 128), 0) // 8 % 16
    lane = lax.broadcasted_iota(jnp.int32, (256, 128), 1)
    plane = ((y - row // 4) % 4 * 2 + (h ^ (1 - row // 2 % 2))) * 2 + row % 2
    placed = jnp.where(lane == plane, sums, 0.0)
    rows = [jnp.sum(placed[p * 128 : p * 128 + 128], axis=0, keepdims=True) for p in range(2)]
    rows.append(jnp.zeros((6, 128), F32))
    out[...] = jnp.concatenate(rows, axis=0) * (1.0 / 32768.0)


def gram(*blocks):
    vmem = pl.BlockSpec(memory_space=pltpu.VMEM)
    return pl.pallas_call(
        gram_kernel,
        out_shape=jax.ShapeDtypeStruct((8, 128), F32),
        in_specs=[vmem] * 4,
        out_specs=vmem,
        compiler_params=pltpu.CompilerParams(vmem_limit_bytes=4 << 20),
        cost_estimate=pl.CostEstimate(flops=1 << 20, bytes_accessed=1 << 18, transcendentals=0),
    )(*blocks)


def arrange_kernel(one, other, out):
    core = lax.axis_index("gz") % 2
    block = jnp.where(core == 1, one[...], other[...])
    block = jnp.where(core == 1, pltpu.roll(block, 112, 1), block)
    for p in range(2):
        for half in range(2):
            at = p * 32 + half * 16
            for q in range(4):
                out[:, p, half * 4 + q, :] = block[at : at + 16, q * 32 : q * 32 + 16]


def arrange(one, other):
    vmem = pl.BlockSpec(memory_space=pltpu.VMEM)
    return pl.pallas_call(
        arrange_kernel,
        out_shape=jax.ShapeDtypeStruct((16, 2, 8, 16), F32),
        in_specs=[vmem, vmem],
        out_specs=vmem,
        compiler_params=pltpu.CompilerParams(vmem_limit_bytes=4 << 20),
        cost_estimate=pl.CostEstimate(flops=1 << 16, bytes_accessed=1 << 18, transcendentals=0),
    )(one, other)


CHIPS = [(y, h, x, z) for y in range(4) for h in range(2) for x in range(4) for z in range(2)]


def index(y, h, x, z, core):
    return (y * 2 + h) * 16 + x * 4 + z * 2 + core


def swap(v):
    pairs = [(index(*chip, c), index(*chip, 1 - c)) for chip in CHIPS for c in range(2)]
    return lax.ppermute(v, AXES, pairs)


def send(v, core, to):
    pairs = []
    for chip in CHIPS:
        pairs.append((index(*chip, core), index(*to(*chip), 1 - core)))
        pairs.append((index(*chip, 1 - core), index(*chip, core)))
    return lax.ppermute(v, AXES, pairs)


def over_z(y, h, x, z):
    return y, h, x, 1 - z


def over_h(y, h, x, z):
    return y, 1 - h, x, z


def over_x(k):
    return lambda y, h, x, z: (y, h, (x + k) % 4, z)


def over_y(k):
    return lambda y, h, x, z: ((y + k) % 4, h, x, z)


def on_device(field_window, second_factor, third_factor, species_factor):
    part = project(field_window, second_factor.T, third_factor.T, species_factor.T)
    with jax.named_scope("reduce"):
        part = part + swap(part)
        far = send(part[256:], 0, over_z)
        part = far + swap(part[:256])
        far = [send(part[64 * k : 64 * k + 64], 1, over_x(k)) for k in (2, 1, 3)]
        block = far[0] + far[1] + far[2] + swap(part[:64])
    with jax.named_scope("gather"):
        far = send(block, 0, over_h)
        mine = swap(block)
        near = jnp.concatenate([far, mine])
        two, one, three = [send(near, 1, over_y(k)) for k in (2, 1, 3)]
        near = swap(near)
    arranged = arrange(mine, block)
    arranged, two = lax.optimization_barrier((arranged, two))
    with jax.named_scope("gram"):
        total = gram(two, one, three, near)
        far = [send(total, 0, over_x(k)) for k in (2, 1, 3)]
        total = far[0] + far[1] + far[2] + swap(total)
        far = send(total, 1, over_z)
        total = far + swap(total)
        mine = swap(total)
        mode_gram = jnp.where(lax.axis_index("gz") % 2 == 0, total, mine)[:2, :16]
    return (jnp.transpose(arranged, (0, 3, 1, 2)), mode_gram)


def solution(mesh):
    in_specs = (P("gx", None, "gy", "gz"), P("gy", None), P("gz", None), P())
    out_specs = (P("gy", "gz", "gx", None), P("gx", None))
    return jax.shard_map(
        on_device, mesh=mesh, in_specs=in_specs, out_specs=out_specs, check_vma=False
    )
```

```python
import jax
import jax.numpy as jnp
from jax import lax
from jax.experimental import pallas as pl
from jax.experimental.pallas import tpu as pltpu
from jax.sharding import PartitionSpec as P

HIGHEST = lax.Precision.HIGHEST
F32 = jnp.float32
BF16 = jnp.bfloat16
AXES = ("gx", "gy", "gz")
ROWS = 32


def split(v):
    high = v.astype(BF16)
    return high, (v - high.astype(F32)).astype(BF16)


def dot(a, b):
    return jnp.dot(a, b, preferred_element_type=F32)


def mask(shape, f):
    i = lax.broadcasted_iota(jnp.int32, shape, 0)
    j = lax.broadcasted_iota(jnp.int32, shape, 1)
    return jnp.where(f(i, j), 1.0, 0.0).astype(F32)


def project_kernel(
    field, second_hbm, third_hbm, species_hbm, out, window, spread, high, low,
    second, third, species, sems, factor_sems,
):
    planes, count, rows, columns = field.shape
    per = rows // ROWS

    def copy(c):
        p, k = c // per, c % per
        return pltpu.make_async_copy(
            field.at[p, :, pl.ds(k * ROWS, ROWS), :], window.at[c], sems.at[c]
        )

    factors = [
        pltpu.make_async_copy(source, target, factor_sems.at[i])
        for i, (source, target) in enumerate(
            ((species_hbm, species), (second_hbm, second), (third_hbm, third))
        )
    ]
    for factor in factors:
        factor.start()
    for c in range(2):
        copy(c).start()
    for factor in factors:
        factor.wait()
    for c in range(2, planes * per):
        copy(c).start()
    x = lax.axis_index("gy")
    z = lax.axis_index("gz") // 2

    r_of = mask((64, 8), lambda i, j: i // 8 == j)
    s_of = mask((32, 256), lambda i, j: j // 8 == i)
    w = jnp.dot(jnp.dot(r_of, species[...], precision=HIGHEST), s_of, precision=HIGHEST)
    w_high, w_low = split(w * mask((64, 256), lambda i, j: i % 8 == j % 8))
    spread[0:64] = w_high
    spread[64:128] = w_low

    def rank_second(i):
        return (x + i // 16) % 4 * 16 + i % 16

    u = jnp.dot(mask((64, 64), lambda i, j: rank_second(i) == j), second[...], precision=HIGHEST)
    u_high, u_low = split(u)
    u_both = jnp.concatenate([u_high, u_low], axis=0)

    pick = mask((256, 64), lambda i, j: j == jnp.where(i // 128 == 0, z, 1 - z) * 32 + i % 32)
    v = lax.dot_general(third[...], pick, (((0,), (1,)), ((), ())), precision=HIGHEST)
    v_high, v_low = split(v)
    lane = lax.broadcasted_iota(jnp.int32, (64, 256), 1) % 128 // 32

    for p in range(planes):

        def step(k, carry, p=p):
            c = p * per + k
            copy(c).wait()
            w_both = spread[...]
            for g in range(ROWS // 16):
                parts = []
                for h in range(2):
                    f = window[c, :, g * 16 + h * 8 : g * 16 + h * 8 + 8, :]
                    f_high, f_low = split(f.reshape(count * 8, columns))
                    d = dot(w_both, f_high)
                    d = d[:64] + d[64:] + dot(w_both[:64], f_low)
                    parts.append(d.reshape(8, 8, columns))
                r_high, r_low = split(jnp.concatenate(parts, axis=1))
                at = pl.ds(pl.multiple_of(k * ROWS + g * 16, 16), 16)
                high[:, at, :] = r_high
                low[:, at, :] = r_low
            return carry

        lax.fori_loop(0, per, step, 0)
        for half in range(2):
            total = jnp.zeros((64, 256), F32)
            for q in range(4):
                r = half * 4 + q
                d = dot(u_both, high[r])
                t_high, t_low = split(d[:64] + d[64:] + dot(u_high, low[r]))
                e = dot(jnp.concatenate([t_high, t_low], axis=0), v_high)
                total = jnp.where(lane == q, e[:64] + e[64:] + dot(t_high, v_low), total)
            for zs in range(2):
                for xs in range(4):
                    at = zs * 256 + xs * 64 + p * 32 + half * 16
                    out[at : at + 16, :] = total[xs * 16 : xs * 16 + 16, zs * 128 : zs * 128 + 128]


def project(field, second, third, species):
    planes, count, rows, columns = field.shape
    vmem = pl.BlockSpec(memory_space=pltpu.VMEM)
    pieces = planes * rows // ROWS
    return pl.pallas_call(
        project_kernel,
        out_shape=pltpu.VMEM((512, 128), F32),
        in_specs=[pl.BlockSpec(memory_space=pltpu.HBM)] * 4,
        out_specs=vmem,
        scratch_shapes=[
            pltpu.VMEM((pieces, count, ROWS, columns), F32),
            pltpu.VMEM((128, 256), BF16),
            pltpu.VMEM((8, rows, columns), BF16),
            pltpu.VMEM((8, rows, columns), BF16),
            pltpu.VMEM(second.shape, F32),
            pltpu.VMEM(third.shape, F32),
            pltpu.VMEM(species.shape, F32),
            pltpu.SemaphoreType.DMA((pieces,)),
            pltpu.SemaphoreType.DMA((3,)),
        ],
        compiler_params=pltpu.CompilerParams(vmem_limit_bytes=48 << 20),
        cost_estimate=pl.CostEstimate(
            flops=1 << 32, bytes_accessed=17 << 20, transcendentals=0
        ),
    )(field, *[pltpu.with_memory_space_constraint(v, pltpu.HBM) for v in (second, third, species)])


def gram_kernel(two, one, three, mine, out):
    gx = lax.axis_index("gx")
    y, h = gx // 2, gx % 2
    sums = []
    for p in range(2):
        own = mine[64 + p * 32 : 96 + p * 32, :]
        for ref in (mine, one, two, three):
            for m in range(4):
                product = own * ref[m * 32 : m * 32 + 32, :]
                sums.append(product[0:8] + product[8:16] + product[16:24] + product[24:32])
    sums = jnp.sum(jnp.concatenate(sums, axis=0), axis=1, keepdims=True)
    row = lax.broadcasted_iota(jnp.int32, (256, 128), 0) // 8 % 16
    lane = lax.broadcasted_iota(jnp.int32, (256, 128), 1)
    plane = ((y - row // 4) % 4 * 2 + (h ^ (1 - row // 2 % 2))) * 2 + row % 2
    placed = jnp.where(lane == plane, sums, 0.0)
    rows = [jnp.sum(placed[p * 128 : p * 128 + 128], axis=0, keepdims=True) for p in range(2)]
    rows.append(jnp.zeros((6, 128), F32))
    out[...] = jnp.concatenate(rows, axis=0) * (1.0 / 32768.0)


def gram(*blocks):
    vmem = pl.BlockSpec(memory_space=pltpu.VMEM)
    return pl.pallas_call(
        gram_kernel,
        out_shape=jax.ShapeDtypeStruct((8, 128), F32),
        in_specs=[vmem] * 4,
        out_specs=vmem,
        compiler_params=pltpu.CompilerParams(vmem_limit_bytes=4 << 20),
        cost_estimate=pl.CostEstimate(flops=1 << 20, bytes_accessed=1 << 18, transcendentals=0),
    )(*blocks)


def arrange_kernel(one, other, out):
    core = lax.axis_index("gz") % 2
    block = jnp.where(core == 1, one[...], other[...])
    block = jnp.where(core == 1, pltpu.roll(block, 112, 1), block)
    for p in range(2):
        for half in range(2):
            at = p * 32 + half * 16
            for q in range(4):
                out[:, p, half * 4 + q, :] = block[at : at + 16, q * 32 : q * 32 + 16]


def arrange(one, other):
    vmem = pl.BlockSpec(memory_space=pltpu.VMEM)
    return pl.pallas_call(
        arrange_kernel,
        out_shape=jax.ShapeDtypeStruct((16, 2, 8, 16), F32),
        in_specs=[vmem, vmem],
        out_specs=vmem,
        compiler_params=pltpu.CompilerParams(vmem_limit_bytes=4 << 20),
        cost_estimate=pl.CostEstimate(flops=1 << 16, bytes_accessed=1 << 18, transcendentals=0),
    )(one, other)


CHIPS = [(y, h, x, z) for y in range(4) for h in range(2) for x in range(4) for z in range(2)]


def index(y, h, x, z, core):
    return (y * 2 + h) * 16 + x * 4 + z * 2 + core


def swap(v):
    pairs = [(index(*chip, c), index(*chip, 1 - c)) for chip in CHIPS for c in range(2)]
    return lax.ppermute(v, AXES, pairs)


def send(v, core, to):
    pairs = []
    for chip in CHIPS:
        pairs.append((index(*chip, core), index(*to(*chip), 1 - core)))
        pairs.append((index(*chip, 1 - core), index(*chip, core)))
    return lax.ppermute(v, AXES, pairs)


def together(*values):
    return lax.optimization_barrier(values)


def over_z(y, h, x, z):
    return y, h, x, 1 - z


def over_h(y, h, x, z):
    return y, 1 - h, x, z


def over_x(k):
    return lambda y, h, x, z: (y, h, (x + k) % 4, z)


def over_y(k):
    return lambda y, h, x, z: ((y + k) % 4, h, x, z)


def on_device(field_window, second_factor, third_factor, species_factor):
    part = project(field_window, second_factor.T, third_factor.T, species_factor.T)
    with jax.named_scope("reduce"):
        part = part + swap(part)
        part = sum(together(send(part[256:], 0, over_z), swap(part[:256])))
        terms = [send(part[64 * k : 64 * k + 64], 1, over_x(k)) for k in (2, 1, 3)]
        terms = together(*terms, swap(part[:64]))
        block = ((terms[0] + terms[1]) + terms[2]) + terms[3]
    with jax.named_scope("gather"):
        far, mine = together(send(block, 0, over_h), swap(block))
        near = jnp.concatenate([far, mine])
        blocks = [send(near, 1, over_y(k)) for k in (2, 1, 3)]
        blocks = [*blocks, swap(near)]
        arranged, blocks[0] = together(arrange(mine, block), blocks[0])
    with jax.named_scope("gram"):
        total = gram(*blocks)
        terms = [send(total, 0, over_x(k)) for k in (2, 1, 3)]
        terms = together(*terms, swap(total))
        total = ((terms[0] + terms[1]) + terms[2]) + terms[3]
        far, mine = together(send(total, 1, over_z), swap(total))
        total = far + mine
        mine = swap(total)
        mode_gram = jnp.where(lax.axis_index("gz") % 2 == 0, total, mine)[:2, :16]
    return (jnp.transpose(arranged, (0, 3, 1, 2)), mode_gram)


def solution(mesh):
    in_specs = (P("gx", None, "gy", "gz"), P("gy", None), P("gz", None), P())
    out_specs = (P("gy", "gz", "gx", None), P("gx", None))
    return jax.shard_map(
        on_device, mesh=mesh, in_specs=in_specs, out_specs=out_specs, check_vma=False
    )
```

```python
import jax
import jax.numpy as jnp
from jax import lax
from jax.experimental import pallas as pl
from jax.experimental.pallas import tpu as pltpu
from jax.sharding import PartitionSpec as P

HIGHEST = lax.Precision.HIGHEST
F32 = jnp.float32
BF16 = jnp.bfloat16
AXES = ("gx", "gy", "gz")
ROWS = 64
REGION = 64


def split(v):
    high = v.astype(BF16)
    return high, (v - high.astype(F32)).astype(BF16)


def dot(a, b):
    return jnp.dot(a, b, preferred_element_type=F32)


def mask(shape, f):
    i = lax.broadcasted_iota(jnp.int32, shape, 0)
    j = lax.broadcasted_iota(jnp.int32, shape, 1)
    return jnp.where(f(i, j), 1.0, 0.0).astype(F32)


def project_kernel(
    field, second_hbm, third_hbm, species_hbm, out, window, spread, v_both, high, low,
    second, third, species, sems, factor_sems,
):
    planes, count, rows, columns = field.shape
    per = rows // ROWS

    def copy(c):
        p, k = c // per, c % per
        return pltpu.make_async_copy(
            field.at[p, :, pl.ds(k * ROWS, ROWS), :], window.at[c], sems.at[c]
        )

    factors = [
        pltpu.make_async_copy(source, target, factor_sems.at[i])
        for i, (source, target) in enumerate(
            ((species_hbm, species), (second_hbm, second), (third_hbm, third))
        )
    ]
    for factor in factors:
        factor.start()
    for c in range(2):
        copy(c).start()
    for factor in factors:
        factor.wait()
    for c in range(2, planes * per):
        copy(c).start()
    x = lax.axis_index("gy")
    given = lax.axis_index("gz") // 2 ^ lax.axis_index("gz") % 2

    r_of = mask((64, 8), lambda i, j: i // 8 == j)
    s_of = mask((32, 256), lambda i, j: j // 8 == i)
    w = jnp.dot(jnp.dot(r_of, species[...], precision=HIGHEST), s_of, precision=HIGHEST)
    w_high, w_low = split(w * mask((64, 256), lambda i, j: i % 8 == j % 8))
    spread[0:64] = w_high
    spread[64:128] = w_low

    def rank_second(i):
        return (x + i // 16) % 4 * 16 + i % 16

    u = jnp.dot(mask((64, 64), lambda i, j: rank_second(i) == j), second[...], precision=HIGHEST)
    u_high, u_low = split(u)
    u_both = jnp.concatenate([u_high, u_low], axis=0)

    pick = mask((256, 64), lambda i, j: j == (given ^ i // 128) * 32 + i % 32)
    v = lax.dot_general(third[...], pick, (((0,), (1,)), ((), ())), precision=HIGHEST)
    v_both[0], v_both[1] = split(v)
    lane = lax.broadcasted_iota(jnp.int32, (64, 256), 1) % 128 // 32

    for p in range(planes):

        def step(k, carry, p=p):
            first = p * per + k * (REGION // ROWS)
            for c in range(REGION // ROWS):
                copy(first + c).wait()
            w_both = spread[...]
            for g in range(REGION // 16):
                parts = []
                for h in range(2):
                    at = g * 16 + h * 8
                    f = window[first + at // ROWS, :, at % ROWS : at % ROWS + 8, :]
                    f_high, f_low = split(f.reshape(count * 8, columns))
                    d = dot(w_both, f_high)
                    d = d[:64] + d[64:] + dot(w_both[:64], f_low)
                    parts.append(d.reshape(8, 8, columns))
                r_high, r_low = split(jnp.concatenate(parts, axis=1))
                at = pl.ds(pl.multiple_of(k * REGION + g * 16, 16), 16)
                high[:, at, :] = r_high
                low[:, at, :] = r_low
            return carry

        lax.fori_loop(0, rows // REGION, step, 0)
        ts = []
        for r in range(8):
            d = dot(u_both, high[r])
            ts.append(d[:64] + d[64:] + dot(u_both[:64], low[r]))
        t_high, t_low = split(jnp.concatenate(ts, axis=0))
        e = dot(jnp.concatenate([t_high, t_low], axis=0), v_both[0])
        e = (e[:512] + e[512:] + dot(t_high, v_both[1])).reshape(8, 64, 256)
        for half in range(2):
            total = e[half * 4]
            for q in range(1, 4):
                total = jnp.where(lane == q, e[half * 4 + q], total)
            for zs in range(2):
                for xs in range(4):
                    at = zs * 256 + xs * 64 + p * 32 + half * 16
                    out[at : at + 16, :] = total[xs * 16 : xs * 16 + 16, zs * 128 : zs * 128 + 128]


def project(field, second, third, species):
    planes, count, rows, columns = field.shape
    vmem = pl.BlockSpec(memory_space=pltpu.VMEM)
    pieces = planes * rows // ROWS
    return pl.pallas_call(
        project_kernel,
        out_shape=pltpu.VMEM((512, 128), F32),
        in_specs=[pl.BlockSpec(memory_space=pltpu.HBM)] * 4,
        out_specs=vmem,
        scratch_shapes=[
            pltpu.VMEM((pieces, count, ROWS, columns), F32),
            pltpu.VMEM((128, 256), BF16),
            pltpu.VMEM((2, columns, 256), BF16),
            pltpu.VMEM((8, rows, columns), BF16),
            pltpu.VMEM((8, rows, columns), BF16),
            pltpu.VMEM(second.shape, F32),
            pltpu.VMEM(third.shape, F32),
            pltpu.VMEM(species.shape, F32),
            pltpu.SemaphoreType.DMA((pieces,)),
            pltpu.SemaphoreType.DMA((3,)),
        ],
        compiler_params=pltpu.CompilerParams(vmem_limit_bytes=48 << 20),
        cost_estimate=pl.CostEstimate(
            flops=1 << 32, bytes_accessed=17 << 20, transcendentals=0
        ),
    )(field, *[pltpu.with_memory_space_constraint(v, pltpu.HBM) for v in (second, third, species)])


def gram_kernel(two, mine, one, three, out):
    gx = lax.axis_index("gx")
    y, h = gx // 2, gx % 2
    sums = []
    for p in range(2):
        own = mine[64 + p * 32 : 96 + p * 32, :]
        for ref in (mine, one, two, three):
            for m in range(4):
                product = own * ref[m * 32 : m * 32 + 32, :]
                sums.append(product[0:8] + product[8:16] + product[16:24] + product[24:32])
    sums = jnp.sum(jnp.concatenate(sums, axis=0), axis=1, keepdims=True)
    row = lax.broadcasted_iota(jnp.int32, (256, 128), 0) // 8 % 16
    lane = lax.broadcasted_iota(jnp.int32, (256, 128), 1)
    plane = ((y - row // 4) % 4 * 2 + (h ^ (1 - row // 2 % 2))) * 2 + row % 2
    placed = jnp.where(lane == plane, sums, 0.0)
    rows = [jnp.sum(placed[p * 128 : p * 128 + 128], axis=0, keepdims=True) for p in range(2)]
    rows.append(jnp.zeros((6, 128), F32))
    out[...] = jnp.concatenate(rows, axis=0) * (1.0 / 32768.0)


def gram(*blocks):
    vmem = pl.BlockSpec(memory_space=pltpu.VMEM)
    return pl.pallas_call(
        gram_kernel,
        out_shape=jax.ShapeDtypeStruct((8, 128), F32),
        in_specs=[vmem] * 4,
        out_specs=vmem,
        compiler_params=pltpu.CompilerParams(vmem_limit_bytes=4 << 20),
        cost_estimate=pl.CostEstimate(flops=1 << 20, bytes_accessed=1 << 18, transcendentals=0),
    )(*blocks)


def arrange_kernel(one, other, out):
    core = lax.axis_index("gz") % 2
    block = jnp.where(core == 1, one[...], other[...])
    block = jnp.where(core == 1, pltpu.roll(block, 112, 1), block)
    for p in range(2):
        for half in range(2):
            at = p * 32 + half * 16
            for q in range(4):
                out[:, p, half * 4 + q, :] = block[at : at + 16, q * 32 : q * 32 + 16]


def arrange(one, other):
    vmem = pl.BlockSpec(memory_space=pltpu.VMEM)
    return pl.pallas_call(
        arrange_kernel,
        out_shape=jax.ShapeDtypeStruct((16, 2, 8, 16), F32),
        in_specs=[vmem, vmem],
        out_specs=vmem,
        compiler_params=pltpu.CompilerParams(vmem_limit_bytes=4 << 20),
        cost_estimate=pl.CostEstimate(flops=1 << 16, bytes_accessed=1 << 18, transcendentals=0),
    )(one, other)


CHIPS = [(y, h, x, z) for y in range(4) for h in range(2) for x in range(4) for z in range(2)]


def index(y, h, x, z, core):
    return (y * 2 + h) * 16 + x * 4 + z * 2 + core


def swap(v):
    pairs = [(index(*chip, c), index(*chip, 1 - c)) for chip in CHIPS for c in range(2)]
    return lax.ppermute(v, AXES, pairs)


def send(v, core, to):
    pairs = []
    for chip in CHIPS:
        pairs.append((index(*chip, core), index(*to(*chip), 1 - core)))
        pairs.append((index(*chip, 1 - core), index(*chip, core)))
    return lax.ppermute(v, AXES, pairs)


def together(*values):
    return lax.optimization_barrier(values)


def over_z(y, h, x, z):
    return y, h, x, 1 - z


def over_h(y, h, x, z):
    return y, 1 - h, x, z


def over_x(k):
    return lambda y, h, x, z: (y, h, (x + k) % 4, z)


def over_y(k):
    return lambda y, h, x, z: ((y + k) % 4, h, x, z)


def on_device(field_window, second_factor, third_factor, species_factor):
    part = project(field_window, second_factor.T, third_factor.T, species_factor.T)
    with jax.named_scope("reduce"):
        part = part[256:] + swap(part[:256])
        part = send(part, 0, over_z) + part
        terms = [send(part[64 * k : 64 * k + 64], 1, over_x(k)) for k in (2, 1, 3)]
        terms = together(*terms, swap(part[:64]))
        block = ((terms[0] + terms[1]) + terms[2]) + terms[3]
    with jax.named_scope("gather"):
        far, mine = together(send(block, 0, over_h), swap(block))
        near = jnp.concatenate([far, mine])
        two, one, three = [send(near, 1, over_y(k)) for k in (2, 1, 3)]
        near = swap(near)
        arranged, two = together(arrange(mine, block), two)
    with jax.named_scope("gram"):
        total = gram(two, near, one, three)
        terms = [send(total, 0, over_x(k)) for k in (2, 1, 3)]
        terms = together(*terms, swap(total))
        total = ((terms[0] + terms[1]) + terms[2]) + terms[3]
        far, mine = together(send(total, 1, over_z), swap(total))
        total = far + mine
        mine = swap(total)
        mode_gram = jnp.where(lax.axis_index("gz") % 2 == 0, total, mine)[:2, :16]
    return (jnp.transpose(arranged, (0, 3, 1, 2)), mode_gram)


def solution(mesh):
    in_specs = (P("gx", None, "gy", "gz"), P("gy", None), P("gz", None), P())
    out_specs = (P("gy", "gz", "gx", None), P("gx", None))
    return jax.shard_map(
        on_device, mesh=mesh, in_specs=in_specs, out_specs=out_specs, check_vma=False
    )
```

```python
import jax
import jax.numpy as jnp
from jax import lax
from jax.experimental import pallas as pl
from jax.experimental.pallas import tpu as pltpu
from jax.sharding import PartitionSpec as P

HIGHEST = lax.Precision.HIGHEST
F32 = jnp.float32
BF16 = jnp.bfloat16
AXES = ("gx", "gy", "gz")
ROWS = 64
REGION = 64


def split(v):
    high = v.astype(BF16)
    return high, (v - high.astype(F32)).astype(BF16)


def dot(a, b):
    return jnp.dot(a, b, preferred_element_type=F32)


def mask(shape, f):
    i = lax.broadcasted_iota(jnp.int32, shape, 0)
    j = lax.broadcasted_iota(jnp.int32, shape, 1)
    return jnp.where(f(i, j), 1.0, 0.0).astype(F32)


def project_kernel(
    field, second_hbm, third_hbm, species_hbm, out, window, spread, v_both, high, low,
    second, third, species, sems, factor_sems,
):
    planes, count, rows, columns = field.shape
    per = rows // ROWS

    def copy(c):
        p, k = c // per, c % per
        return pltpu.make_async_copy(
            field.at[p, :, pl.ds(k * ROWS, ROWS), :], window.at[c], sems.at[c]
        )

    factors = [
        pltpu.make_async_copy(source, target, factor_sems.at[i])
        for i, (source, target) in enumerate(
            ((species_hbm, species), (second_hbm, second), (third_hbm, third))
        )
    ]
    for factor in factors:
        factor.start()
    for c in range(2):
        copy(c).start()
    for factor in factors:
        factor.wait()
    for c in range(2, planes * per):
        copy(c).start()
    x = lax.axis_index("gy")
    given = lax.axis_index("gz") // 2 ^ lax.axis_index("gz") % 2

    r_of = mask((64, 8), lambda i, j: i // 8 == j)
    s_of = mask((32, 256), lambda i, j: j // 8 == i)
    w = jnp.dot(jnp.dot(r_of, species[...], precision=HIGHEST), s_of, precision=HIGHEST)
    w_high, w_low = split(w * mask((64, 256), lambda i, j: i % 8 == j % 8))
    spread[0:64] = w_high
    spread[64:128] = w_low

    def rank_second(i):
        return (x + i // 16) % 4 * 16 + i % 16

    u = jnp.dot(mask((64, 64), lambda i, j: rank_second(i) == j), second[...], precision=HIGHEST)
    u_high, u_low = split(u)
    u_both = jnp.concatenate([u_high, u_low], axis=0)

    pick = mask((256, 64), lambda i, j: j == (given ^ i // 128) * 32 + i % 32)
    v = lax.dot_general(third[...], pick, (((0,), (1,)), ((), ())), precision=HIGHEST)
    v_both[0], v_both[1] = split(v)
    lane = lax.broadcasted_iota(jnp.int32, (64, 256), 1) % 128 // 32

    for p in range(planes):

        def step(k, carry, p=p):
            first = p * per + k * (REGION // ROWS)
            for c in range(REGION // ROWS):
                copy(first + c).wait()
            w_both = spread[...]
            for g in range(REGION // 16):
                parts = []
                for h in range(2):
                    at = g * 16 + h * 8
                    f = window[first + at // ROWS, :, at % ROWS : at % ROWS + 8, :]
                    f_high, f_low = split(f.reshape(count * 8, columns))
                    d = dot(w_both, f_high)
                    d = d[:64] + d[64:] + dot(w_both[:64], f_low)
                    parts.append(d.reshape(8, 8, columns))
                r_high, r_low = split(jnp.concatenate(parts, axis=1))
                at = pl.ds(pl.multiple_of(k * REGION + g * 16, 16), 16)
                high[:, at, :] = r_high
                low[:, at, :] = r_low
            return carry

        lax.fori_loop(0, rows // REGION, step, 0)
        ts = []
        for r in range(8):
            d = dot(u_both, high[r])
            ts.append(d[:64] + d[64:] + dot(u_both[:64], low[r]))
        t_high, t_low = split(jnp.concatenate(ts, axis=0))
        e = dot(jnp.concatenate([t_high, t_low], axis=0), v_both[0])
        e = (e[:512] + e[512:] + dot(t_high, v_both[1])).reshape(8, 64, 256)
        for half in range(2):
            total = e[half * 4]
            for q in range(1, 4):
                total = jnp.where(lane == q, e[half * 4 + q], total)
            for zs in range(2):
                for xs in range(4):
                    at = zs * 256 + xs * 64 + p * 32 + half * 16
                    out[at : at + 16, :] = total[xs * 16 : xs * 16 + 16, zs * 128 : zs * 128 + 128]


def project(field, second, third, species):
    planes, count, rows, columns = field.shape
    vmem = pl.BlockSpec(memory_space=pltpu.VMEM)
    pieces = planes * rows // ROWS
    return pl.pallas_call(
        project_kernel,
        out_shape=pltpu.VMEM((512, 128), F32),
        in_specs=[pl.BlockSpec(memory_space=pltpu.HBM)] * 4,
        out_specs=vmem,
        scratch_shapes=[
            pltpu.VMEM((pieces, count, ROWS, columns), F32),
            pltpu.VMEM((128, 256), BF16),
            pltpu.VMEM((2, columns, 256), BF16),
            pltpu.VMEM((8, rows, columns), BF16),
            pltpu.VMEM((8, rows, columns), BF16),
            pltpu.VMEM(second.shape, F32),
            pltpu.VMEM(third.shape, F32),
            pltpu.VMEM(species.shape, F32),
            pltpu.SemaphoreType.DMA((pieces,)),
            pltpu.SemaphoreType.DMA((3,)),
        ],
        compiler_params=pltpu.CompilerParams(vmem_limit_bytes=48 << 20),
        cost_estimate=pl.CostEstimate(
            flops=1 << 32, bytes_accessed=17 << 20, transcendentals=0
        ),
    )(field, *[pltpu.with_memory_space_constraint(v, pltpu.HBM) for v in (second, third, species)])


def gram_kernel(two, mine, one, three, out):
    gx = lax.axis_index("gx")
    y, h = gx // 2, gx % 2
    sums = []
    for p in range(2):
        own = mine[64 + p * 32 : 96 + p * 32, :]
        for ref in (mine, one, two, three):
            for m in range(4):
                product = own * ref[m * 32 : m * 32 + 32, :]
                sums.append(product[0:8] + product[8:16] + product[16:24] + product[24:32])
    sums = jnp.sum(jnp.concatenate(sums, axis=0), axis=1, keepdims=True)
    row = lax.broadcasted_iota(jnp.int32, (256, 128), 0) // 8 % 16
    lane = lax.broadcasted_iota(jnp.int32, (256, 128), 1)
    plane = ((y - row // 4) % 4 * 2 + (h ^ (1 - row // 2 % 2))) * 2 + row % 2
    placed = jnp.where(lane == plane, sums, 0.0)
    rows = [jnp.sum(placed[p * 128 : p * 128 + 128], axis=0, keepdims=True) for p in range(2)]
    rows.append(jnp.zeros((6, 128), F32))
    out[...] = jnp.concatenate(rows, axis=0) * (1.0 / 32768.0)


def gram(*blocks):
    vmem = pl.BlockSpec(memory_space=pltpu.VMEM)
    return pl.pallas_call(
        gram_kernel,
        out_shape=jax.ShapeDtypeStruct((8, 128), F32),
        in_specs=[vmem] * 4,
        out_specs=vmem,
        compiler_params=pltpu.CompilerParams(vmem_limit_bytes=4 << 20),
        cost_estimate=pl.CostEstimate(flops=1 << 20, bytes_accessed=1 << 18, transcendentals=0),
    )(*blocks)


def arrange_kernel(one, other, out):
    core = lax.axis_index("gz") % 2
    block = jnp.where(core == 1, one[...], other[...])
    block = jnp.where(core == 1, pltpu.roll(block, 112, 1), block)
    for p in range(2):
        for half in range(2):
            at = p * 32 + half * 16
            for q in range(4):
                out[:, p, half * 4 + q, :] = block[at : at + 16, q * 32 : q * 32 + 16]


def arrange(one, other):
    vmem = pl.BlockSpec(memory_space=pltpu.VMEM)
    return pl.pallas_call(
        arrange_kernel,
        out_shape=jax.ShapeDtypeStruct((16, 2, 8, 16), F32),
        in_specs=[vmem, vmem],
        out_specs=vmem,
        compiler_params=pltpu.CompilerParams(vmem_limit_bytes=4 << 20),
        cost_estimate=pl.CostEstimate(flops=1 << 16, bytes_accessed=1 << 18, transcendentals=0),
    )(one, other)


CHIPS = [(y, h, x, z) for y in range(4) for h in range(2) for x in range(4) for z in range(2)]


def index(y, h, x, z, core):
    return (y * 2 + h) * 16 + x * 4 + z * 2 + core


def swap(v):
    pairs = [(index(*chip, c), index(*chip, 1 - c)) for chip in CHIPS for c in range(2)]
    return lax.ppermute(v, AXES, pairs)


def send(v, core, to):
    pairs = []
    for chip in CHIPS:
        pairs.append((index(*chip, core), index(*to(*chip), 1 - core)))
        pairs.append((index(*chip, 1 - core), index(*chip, core)))
    return lax.ppermute(v, AXES, pairs)


def trade(v):
    pairs = [(index(*chip, c), index(*over_z(*chip), c)) for chip in CHIPS for c in range(2)]
    return lax.ppermute(v, AXES, pairs)


def together(*values):
    return lax.optimization_barrier(values)


def over_z(y, h, x, z):
    return y, h, x, 1 - z


def over_h(y, h, x, z):
    return y, 1 - h, x, z


def over_x(k):
    return lambda y, h, x, z: (y, h, (x + k) % 4, z)


def over_y(k):
    return lambda y, h, x, z: ((y + k) % 4, h, x, z)


def on_device(field_window, second_factor, third_factor, species_factor):
    part = project(field_window, second_factor.T, third_factor.T, species_factor.T)
    with jax.named_scope("reduce"):
        part = part[256:] + swap(part[:256])
        part = send(part, 0, over_z) + part
        terms = [send(part[64 * k : 64 * k + 64], 1, over_x(k)) for k in (2, 1, 3)]
        terms = together(*terms, swap(part[:64]))
        block = ((terms[0] + terms[1]) + terms[2]) + terms[3]
    with jax.named_scope("gather"):
        far, mine = together(send(block, 0, over_h), swap(block))
        near = jnp.concatenate([far, mine])
        two, one, three = [send(near, 1, over_y(k)) for k in (2, 1, 3)]
        near = swap(near)
        arranged, two = together(arrange(mine, block), two)
    with jax.named_scope("gram"):
        total = gram(two, near, one, three)
        terms = [send(total, 0, over_x(k)) for k in (2, 1, 3)]
        terms = together(*terms, swap(total))
        total = ((terms[0] + terms[1]) + terms[2]) + terms[3]
        other, far, mine = together(trade(total), send(total, 1, over_z), swap(total))
        first_core = lax.axis_index("gz") % 2 == 0
        mode_gram = jnp.where(first_core, far + mine, total + other)[:2, :16]
    return (jnp.transpose(arranged, (0, 3, 1, 2)), mode_gram)


def solution(mesh):
    in_specs = (P("gx", None, "gy", "gz"), P("gy", None), P("gz", None), P())
    out_specs = (P("gy", "gz", "gx", None), P("gx", None))
    return jax.shard_map(
        on_device, mesh=mesh, in_specs=in_specs, out_specs=out_specs, check_vma=False
    )
```

```python
import jax
import jax.numpy as jnp
from jax import lax
from jax.experimental import pallas as pl
from jax.experimental.pallas import tpu as pltpu
from jax.sharding import PartitionSpec as P

HIGHEST = lax.Precision.HIGHEST
F32 = jnp.float32
BF16 = jnp.bfloat16
AXES = ("gx", "gy", "gz")
ROWS = 64
REGION = 64


def split(v):
    high = v.astype(BF16)
    return high, (v - high.astype(F32)).astype(BF16)


def dot(a, b):
    return jnp.dot(a, b, preferred_element_type=F32)


def mask(shape, f):
    i = lax.broadcasted_iota(jnp.int32, shape, 0)
    j = lax.broadcasted_iota(jnp.int32, shape, 1)
    return jnp.where(f(i, j), 1.0, 0.0).astype(F32)


def project_kernel(
    field, second_hbm, third_hbm, species_hbm, out, window, spread, v_both, high, low,
    second, third, species, sems, factor_sems,
):
    planes, count, rows, columns = field.shape
    per = rows // ROWS

    def copy(c):
        p, k = c // per, c % per
        return pltpu.make_async_copy(
            field.at[p, :, pl.ds(k * ROWS, ROWS), :], window.at[c], sems.at[c]
        )

    factors = [
        pltpu.make_async_copy(source, target, factor_sems.at[i])
        for i, (source, target) in enumerate(
            ((species_hbm, species), (second_hbm, second), (third_hbm, third))
        )
    ]
    for factor in factors:
        factor.start()
    for c in range(2):
        copy(c).start()
    for factor in factors:
        factor.wait()
    for c in range(2, planes * per):
        copy(c).start()
    x = lax.axis_index("gy")
    given = lax.axis_index("gz") // 2 ^ lax.axis_index("gz") % 2 ^ lax.axis_index("gx") % 2

    r_of = mask((64, 8), lambda i, j: i // 8 == j)
    s_of = mask((32, 256), lambda i, j: j // 8 == i)
    w = jnp.dot(jnp.dot(r_of, species[...], precision=HIGHEST), s_of, precision=HIGHEST)
    w_high, w_low = split(w * mask((64, 256), lambda i, j: i % 8 == j % 8))
    spread[0:64] = w_high
    spread[64:128] = w_low

    def rank_second(i):
        return (x + i // 16) % 4 * 16 + i % 16

    u = jnp.dot(mask((64, 64), lambda i, j: rank_second(i) == j), second[...], precision=HIGHEST)
    u_high, u_low = split(u)
    u_both = jnp.concatenate([u_high, u_low], axis=0)

    pick = mask((256, 64), lambda i, j: j == (given ^ i // 128) * 32 + i % 32)
    v = lax.dot_general(third[...], pick, (((0,), (1,)), ((), ())), precision=HIGHEST)
    v_both[0], v_both[1] = split(v)
    lane = lax.broadcasted_iota(jnp.int32, (64, 256), 1) % 128 // 32

    for p in range(planes):

        def step(k, carry, p=p):
            first = p * per + k * (REGION // ROWS)
            for c in range(REGION // ROWS):
                copy(first + c).wait()
            w_both = spread[...]
            for g in range(REGION // 16):
                parts = []
                for h in range(2):
                    at = g * 16 + h * 8
                    f = window[first + at // ROWS, :, at % ROWS : at % ROWS + 8, :]
                    f_high, f_low = split(f.reshape(count * 8, columns))
                    d = dot(w_both, f_high)
                    d = d[:64] + d[64:] + dot(w_both[:64], f_low)
                    parts.append(d.reshape(8, 8, columns))
                r_high, r_low = split(jnp.concatenate(parts, axis=1))
                at = pl.ds(pl.multiple_of(k * REGION + g * 16, 16), 16)
                high[:, at, :] = r_high
                low[:, at, :] = r_low
            return carry

        lax.fori_loop(0, rows // REGION, step, 0)
        ts = []
        for r in range(8):
            d = dot(u_both, high[r])
            ts.append(d[:64] + d[64:] + dot(u_both[:64], low[r]))
        t_high, t_low = split(jnp.concatenate(ts, axis=0))
        e = dot(jnp.concatenate([t_high, t_low], axis=0), v_both[0])
        e = (e[:512] + e[512:] + dot(t_high, v_both[1])).reshape(8, 64, 256)
        for half in range(2):
            total = e[half * 4]
            for q in range(1, 4):
                total = jnp.where(lane == q, e[half * 4 + q], total)
            for zs in range(2):
                for xs in range(4):
                    at = zs * 256 + xs * 64 + p * 32 + half * 16
                    out[at : at + 16, :] = total[xs * 16 : xs * 16 + 16, zs * 128 : zs * 128 + 128]


def project(field, second, third, species):
    planes, count, rows, columns = field.shape
    vmem = pl.BlockSpec(memory_space=pltpu.VMEM)
    pieces = planes * rows // ROWS
    return pl.pallas_call(
        project_kernel,
        out_shape=pltpu.VMEM((512, 128), F32),
        in_specs=[pl.BlockSpec(memory_space=pltpu.HBM)] * 4,
        out_specs=vmem,
        scratch_shapes=[
            pltpu.VMEM((pieces, count, ROWS, columns), F32),
            pltpu.VMEM((128, 256), BF16),
            pltpu.VMEM((2, columns, 256), BF16),
            pltpu.VMEM((8, rows, columns), BF16),
            pltpu.VMEM((8, rows, columns), BF16),
            pltpu.VMEM(second.shape, F32),
            pltpu.VMEM(third.shape, F32),
            pltpu.VMEM(species.shape, F32),
            pltpu.SemaphoreType.DMA((pieces,)),
            pltpu.SemaphoreType.DMA((3,)),
        ],
        compiler_params=pltpu.CompilerParams(vmem_limit_bytes=48 << 20),
        cost_estimate=pl.CostEstimate(
            flops=1 << 32, bytes_accessed=17 << 20, transcendentals=0
        ),
    )(field, *[pltpu.with_memory_space_constraint(v, pltpu.HBM) for v in (second, third, species)])


def gram_kernel(three, mine, two, one, out):
    gx = lax.axis_index("gx")
    y, h = gx // 2, gx % 2
    sums = []
    for p in range(2):
        own = mine[64 + p * 32 : 96 + p * 32, :]
        for ref in (mine, one, two, three):
            for m in range(4):
                product = own * ref[m * 32 : m * 32 + 32, :]
                sums.append(product[0:8] + product[8:16] + product[16:24] + product[24:32])
    sums = jnp.sum(jnp.concatenate(sums, axis=0), axis=1, keepdims=True)
    row = lax.broadcasted_iota(jnp.int32, (256, 128), 0) // 8 % 16
    lane = lax.broadcasted_iota(jnp.int32, (256, 128), 1)
    plane = ((y - row // 4) % 4 * 2 + (h ^ (1 - row // 2 % 2))) * 2 + row % 2
    placed = jnp.where(lane == plane, sums, 0.0)
    rows = [jnp.sum(placed[p * 128 : p * 128 + 128], axis=0, keepdims=True) for p in range(2)]
    rows.append(jnp.zeros((6, 128), F32))
    out[...] = jnp.concatenate(rows, axis=0) * (1.0 / 32768.0)


def gram(*blocks):
    vmem = pl.BlockSpec(memory_space=pltpu.VMEM)
    return pl.pallas_call(
        gram_kernel,
        out_shape=jax.ShapeDtypeStruct((8, 128), F32),
        in_specs=[vmem] * 4,
        out_specs=vmem,
        compiler_params=pltpu.CompilerParams(vmem_limit_bytes=4 << 20),
        cost_estimate=pl.CostEstimate(flops=1 << 20, bytes_accessed=1 << 18, transcendentals=0),
    )(*blocks)


def arrange_kernel(here, there, out):
    core = lax.axis_index("gz") % 2
    block = jnp.where(lax.axis_index("gx") % 2 == 0, here[...], there[...])
    block = jnp.where(core == 1, pltpu.roll(block, 112, 1), block)
    for p in range(2):
        for half in range(2):
            at = p * 32 + half * 16
            for q in range(4):
                out[:, p, half * 4 + q, :] = block[at : at + 16, q * 32 : q * 32 + 16]


def arrange(here, there):
    vmem = pl.BlockSpec(memory_space=pltpu.VMEM)
    return pl.pallas_call(
        arrange_kernel,
        out_shape=jax.ShapeDtypeStruct((16, 2, 8, 16), F32),
        in_specs=[vmem, vmem],
        out_specs=vmem,
        compiler_params=pltpu.CompilerParams(vmem_limit_bytes=4 << 20),
        cost_estimate=pl.CostEstimate(flops=1 << 16, bytes_accessed=1 << 18, transcendentals=0),
    )(here, there)


CHIPS = [(y, h, x, z) for y in range(4) for h in range(2) for x in range(4) for z in range(2)]


def index(y, h, x, z, core):
    return (y * 2 + h) * 16 + x * 4 + z * 2 + core


def swap(v):
    pairs = [(index(*chip, c), index(*chip, 1 - c)) for chip in CHIPS for c in range(2)]
    return lax.ppermute(v, AXES, pairs)


def send(v, core, to):
    pairs = []
    for chip in CHIPS:
        pairs.append((index(*chip, core), index(*to(*chip), 1 - core)))
        pairs.append((index(*chip, 1 - core), index(*chip, core)))
    return lax.ppermute(v, AXES, pairs)


def trade(v):
    pairs = [(index(*chip, c), index(*over_z(*chip), c)) for chip in CHIPS for c in range(2)]
    return lax.ppermute(v, AXES, pairs)


def together(*values):
    return lax.optimization_barrier(values)


def over_z(y, h, x, z):
    return y, h, x, 1 - z


def over_h(y, h, x, z):
    return y, 1 - h, x, 1 - z


def over_x(k):
    return lambda y, h, x, z: (y, h, (x + k) % 4, z)


def over_y(k):
    return lambda y, h, x, z: ((y + k) % 4, h, x, z)


def on_device(field_window, second_factor, third_factor, species_factor):
    part = project(field_window, second_factor.T, third_factor.T, species_factor.T)
    first_core = lax.axis_index("gz") % 2 == 0
    with jax.named_scope("reduce"):
        part = part[256:] + swap(part[:256])
        part = send(part, 0, over_z) + part
        terms = [send(part[64 * k : 64 * k + 64], 1, over_x(k)) for k in (2, 1, 3)]
        terms = together(*terms, swap(part[:64]))
        block = ((terms[0] + terms[1]) + terms[2]) + terms[3]
    with jax.named_scope("gather"):
        far, mine = together(send(block, 0, over_h), swap(block))
        near = jnp.concatenate([far, mine])
        two, one, three = [send(near, 1, over_y(k)) for k in (2, 1, 3)]
        near = swap(near)
    with jax.named_scope("gram"):
        total = gram(three, near, two, one)
        total, here = together(total, jnp.where(first_core, block, mine))
        there = trade(here)
        terms = [send(total, 0, over_x(k)) for k in (2, 1, 3)]
        terms = together(*terms, swap(total))
        total = ((terms[0] + terms[1]) + terms[2]) + terms[3]
        arranged = arrange(here, there)
        other, far, mine, arranged = together(
            trade(total), send(total, 1, over_z), swap(total), arranged
        )
        mode_gram = jnp.where(first_core, far + mine, total + other)[:2, :16]
    return (jnp.transpose(arranged, (0, 3, 1, 2)), mode_gram)


def solution(mesh):
    in_specs = (P("gx", None, "gy", "gz"), P("gy", None), P("gz", None), P())
    out_specs = (P("gy", "gz", "gx", None), P("gx", None))
    return jax.shard_map(
        on_device, mesh=mesh, in_specs=in_specs, out_specs=out_specs, check_vma=False
    )
```

```python
import jax
import jax.numpy as jnp
from jax import lax
from jax.experimental import pallas as pl
from jax.experimental.pallas import tpu as pltpu
from jax.sharding import PartitionSpec as P

HIGHEST = lax.Precision.HIGHEST
F32 = jnp.float32
BF16 = jnp.bfloat16
AXES = ("gx", "gy", "gz")
ROWS = 64


def split(v):
    high = v.astype(BF16)
    return high, (v - high.astype(F32)).astype(BF16)


def dot(a, b):
    return jnp.dot(a, b, preferred_element_type=F32)


def mask(shape, f):
    i = lax.broadcasted_iota(jnp.int32, shape, 0)
    j = lax.broadcasted_iota(jnp.int32, shape, 1)
    return jnp.where(f(i, j), 1.0, 0.0).astype(F32)


def species_step(k, piece, spread, high, low):
    count, _, columns = piece.shape
    w_both = spread[...]
    for g in range(ROWS // 16):
        parts = []
        for at in (g * 16, g * 16 + 8):
            f_high, f_low = split(piece[:, at : at + 8, :].reshape(count * 8, columns))
            d = dot(w_both, f_high)
            d = d[:64] + d[64:] + dot(w_both[:64], f_low)
            parts.append(d.reshape(8, 8, columns))
        r_high, r_low = split(jnp.concatenate(parts, axis=1))
        at = pl.ds(pl.multiple_of(k * ROWS + g * 16, 16), 16)
        high[:, at, :] = r_high
        low[:, at, :] = r_low


def modes(out, high, low, u_both, v_both, last_high=None, last_low=None):
    ts = []
    for r in range(8):
        r_high, r_low = high[r], low[r]
        if last_high is not None:
            r_high = jnp.concatenate([r_high[: -ROWS], last_high[r]], axis=0)
            r_low = jnp.concatenate([r_low[: -ROWS], last_low[r]], axis=0)
        d = dot(u_both[...], r_high)
        ts.append(d[:64] + d[64:] + dot(u_both[0:64], r_low))
    t_high, t_low = split(jnp.concatenate(ts, axis=0))
    e = dot(jnp.concatenate([t_high, t_low], axis=0), v_both[0])
    e = (e[:512] + e[512:] + dot(t_high, v_both[1])).reshape(8, 64, 256)
    lane = lax.broadcasted_iota(jnp.int32, (64, 256), 1) % 128 // 32
    for half in range(2):
        total = e[half * 4]
        for q in range(1, 4):
            total = jnp.where(lane == q, e[half * 4 + q], total)
        for zs in range(2):
            for xs in range(4):
                at = zs * 128 + xs * 32 + half * 16
                out[at : at + 16, :] = total[xs * 16 : xs * 16 + 16, zs * 128 : zs * 128 + 128]


def first_kernel(
    field, second_hbm, third_hbm, species_hbm, out, later, next_high, next_low, spread, u_both, v_both,
    window, high, low, second, third, species, sems, factor_sems,
):
    planes, count, rows, columns = field.shape
    per = rows // ROWS

    last = planes * per - 1

    def copy(c, target=None):
        rows_at = pl.ds(pl.multiple_of(c % per * ROWS, ROWS), ROWS)
        return pltpu.make_async_copy(
            field.at[c // per, :, rows_at, :],
            window.at[c] if target is None else target,
            sems.at[c],
        )

    factors = [
        pltpu.make_async_copy(source, target, factor_sems.at[i])
        for i, (source, target) in enumerate(
            ((species_hbm, species), (second_hbm, second), (third_hbm, third))
        )
    ]
    for factor in factors:
        factor.start()
    for c in range(2):
        copy(c).start()
    for factor in factors:
        factor.wait()
    for c in range(2, last):
        copy(c).start()
    copy(last, later).start()
    x = lax.axis_index("gy")
    given = lax.axis_index("gz") // 2 ^ lax.axis_index("gz") % 2 ^ lax.axis_index("gx") % 2

    r_of = mask((64, 8), lambda i, j: i // 8 == j)
    s_of = mask((32, 256), lambda i, j: j // 8 == i)
    w = jnp.dot(jnp.dot(r_of, species[...], precision=HIGHEST), s_of, precision=HIGHEST)
    spread[0:64], spread[64:128] = split(w * mask((64, 256), lambda i, j: i % 8 == j % 8))

    def rank_second(i):
        return (x + i // 16) % 4 * 16 + i % 16

    u = jnp.dot(mask((64, 64), lambda i, j: rank_second(i) == j), second[...], precision=HIGHEST)
    u_both[0:64], u_both[64:128] = split(u)

    pick = mask((256, 64), lambda i, j: j == (given ^ i // 128) * 32 + i % 32)
    v = lax.dot_general(third[...], pick, (((0,), (1,)), ((), ())), precision=HIGHEST)
    v_both[0], v_both[1] = split(v)

    def step(k, carry):
        copy(k).wait()
        species_step(k, window.at[k], spread, high, low)
        return carry

    def next_step(k, carry):
        copy(per + k).wait()
        species_step(k, window.at[per + k], spread, next_high, next_low)
        return carry

    lax.fori_loop(0, per, step, 0)
    modes(out, high, low, u_both, v_both)
    lax.fori_loop(0, per - 1, next_step, 0)
    copy(last, later).wait()


def second_kernel(later, next_high, next_low, spread, u_both, v_both, out, high, low):
    species_step(0, later, spread, high, low)
    modes(out, next_high, next_low, u_both, v_both, high, low)


def project(field, second, third, species):
    planes, count, rows, columns = field.shape
    vmem = pl.BlockSpec(memory_space=pltpu.VMEM)
    per = rows // ROWS
    one, *kept = pl.pallas_call(
        first_kernel,
        out_shape=[
            pltpu.VMEM((256, 128), F32),
            pltpu.VMEM((count, ROWS, columns), F32),
            pltpu.VMEM((8, rows, columns), BF16),
            pltpu.VMEM((8, rows, columns), BF16),
            pltpu.VMEM((128, 256), BF16),
            pltpu.VMEM((128, 256), BF16),
            pltpu.VMEM((2, columns, 256), BF16),
        ],
        in_specs=[pl.BlockSpec(memory_space=pltpu.HBM)] * 4,
        out_specs=[vmem] * 7,
        scratch_shapes=[
            pltpu.VMEM((planes * per - 1, count, ROWS, columns), F32),
            pltpu.VMEM((8, rows, columns), BF16),
            pltpu.VMEM((8, rows, columns), BF16),
            pltpu.VMEM(second.shape, F32),
            pltpu.VMEM(third.shape, F32),
            pltpu.VMEM(species.shape, F32),
            pltpu.SemaphoreType.DMA((planes * per,)),
            pltpu.SemaphoreType.DMA((3,)),
        ],
        compiler_params=pltpu.CompilerParams(vmem_limit_bytes=32 << 20),
        cost_estimate=pl.CostEstimate(
            flops=1 << 31, bytes_accessed=17 << 20, transcendentals=0
        ),
    )(*[pltpu.with_memory_space_constraint(v, pltpu.HBM) for v in (field, second, third, species)])
    two = pl.pallas_call(
        second_kernel,
        out_shape=pltpu.VMEM((256, 128), F32),
        in_specs=[vmem] * 6,
        out_specs=vmem,
        scratch_shapes=[pltpu.VMEM((8, ROWS, columns), BF16)] * 2,
        compiler_params=pltpu.CompilerParams(vmem_limit_bytes=16 << 20),
        cost_estimate=pl.CostEstimate(
            flops=1 << 31, bytes_accessed=9 << 20, transcendentals=0
        ),
    )(*[pltpu.with_memory_space_constraint(v, pltpu.VMEM) for v in kept])
    return one, two


def gram_kernel(two, one, three, mine, out):
    gx = lax.axis_index("gx")
    y, h = gx // 2, gx % 2
    sums = []
    for p in range(2):
        own = mine[64 + p * 32 : 96 + p * 32, :]
        for ref in (mine, one, two, three):
            for m in range(4):
                product = own * ref[m * 32 : m * 32 + 32, :]
                sums.append(product[0:8] + product[8:16] + product[16:24] + product[24:32])
    sums = jnp.sum(jnp.concatenate(sums, axis=0), axis=1, keepdims=True)
    row = lax.broadcasted_iota(jnp.int32, (256, 128), 0) // 8 % 16
    lane = lax.broadcasted_iota(jnp.int32, (256, 128), 1)
    plane = ((y - row // 4) % 4 * 2 + (h ^ (1 - row // 2 % 2))) * 2 + row % 2
    placed = jnp.where(lane == plane, sums, 0.0)
    rows = [jnp.sum(placed[p * 128 : p * 128 + 128], axis=0, keepdims=True) for p in range(2)]
    rows.append(jnp.zeros((6, 128), F32))
    out[...] = jnp.concatenate(rows, axis=0) * (1.0 / 32768.0)


def gram(*blocks):
    vmem = pl.BlockSpec(memory_space=pltpu.VMEM)
    return pl.pallas_call(
        gram_kernel,
        out_shape=jax.ShapeDtypeStruct((8, 128), F32),
        in_specs=[vmem] * 4,
        out_specs=vmem,
        compiler_params=pltpu.CompilerParams(vmem_limit_bytes=4 << 20),
        cost_estimate=pl.CostEstimate(flops=1 << 20, bytes_accessed=1 << 18, transcendentals=0),
    )(*blocks)


def arrange_kernel(here, there, out):
    core = lax.axis_index("gz") % 2
    block = jnp.where(lax.axis_index("gx") % 2 == 0, here[...], there[...])
    block = jnp.where(core == 1, pltpu.roll(block, 112, 1), block)
    for p in range(2):
        for half in range(2):
            at = p * 32 + half * 16
            for q in range(4):
                out[:, p, half * 4 + q, :] = block[at : at + 16, q * 32 : q * 32 + 16]


def arrange(here, there):
    vmem = pl.BlockSpec(memory_space=pltpu.VMEM)
    return pl.pallas_call(
        arrange_kernel,
        out_shape=jax.ShapeDtypeStruct((16, 2, 8, 16), F32),
        in_specs=[vmem, vmem],
        out_specs=vmem,
        compiler_params=pltpu.CompilerParams(vmem_limit_bytes=4 << 20),
        cost_estimate=pl.CostEstimate(flops=1 << 16, bytes_accessed=1 << 18, transcendentals=0),
    )(here, there)


CHIPS = [(y, h, x, z) for y in range(4) for h in range(2) for x in range(4) for z in range(2)]


def index(y, h, x, z, core):
    return (y * 2 + h) * 16 + x * 4 + z * 2 + core


def swap(v):
    pairs = [(index(*chip, c), index(*chip, 1 - c)) for chip in CHIPS for c in range(2)]
    return lax.ppermute(v, AXES, pairs)


def send(v, core, to):
    pairs = []
    for chip in CHIPS:
        pairs.append((index(*chip, core), index(*to(*chip), 1 - core)))
        pairs.append((index(*chip, 1 - core), index(*chip, core)))
    return lax.ppermute(v, AXES, pairs)


def trade(v):
    pairs = [(index(*chip, c), index(*over_z(*chip), c)) for chip in CHIPS for c in range(2)]
    return lax.ppermute(v, AXES, pairs)


def together(*values):
    return lax.optimization_barrier(values)


def over_z(y, h, x, z):
    return y, h, x, 1 - z


def over_h(y, h, x, z):
    return y, 1 - h, x, 1 - z


def over_x(k):
    return lambda y, h, x, z: (y, h, (x + k) % 4, z)


def over_y(k):
    return lambda y, h, x, z: ((y + k) % 4, h, x, z)


def on_device(field_window, second_factor, third_factor, species_factor):
    one, two = project(field_window, second_factor.T, third_factor.T, species_factor.T)
    first_core = lax.axis_index("gz") % 2 == 0
    with jax.named_scope("reduce"):
        given = swap(one[:128])
        two, given = together(two, given)
        one = one[128:] + given
        far = send(one, 0, over_z)
        two = two[128:] + swap(two[:128])
        parts = [far + one, send(two, 0, over_z) + two]
        pieces = [jnp.concatenate([part[32 * k : 32 * k + 32] for part in parts]) for k in range(4)]
        terms = [swap(pieces[0]), *[send(pieces[k], 1, over_x(k)) for k in (3, 1, 2)]]
        terms = together(*terms)
        block = ((terms[0] + terms[1]) + terms[2]) + terms[3]
    with jax.named_scope("gather"):
        far, mine = together(send(block, 0, over_h), swap(block))
        near = jnp.concatenate([far, mine])
        two, one, three = [send(near, 1, over_y(k)) for k in (2, 1, 3)]
        near = swap(near)
    with jax.named_scope("gram"):
        total = gram(two, one, three, near)
        total, here = together(total, jnp.where(first_core, block, mine))
        there = trade(here)
        terms = [send(total, 0, over_x(k)) for k in (2, 1, 3)]
        terms = together(*terms, swap(total))
        total = ((terms[0] + terms[1]) + terms[2]) + terms[3]
        arranged = arrange(here, there)
        other, far, mine, arranged = together(
            trade(total), send(total, 1, over_z), swap(total), arranged
        )
        mode_gram = jnp.where(first_core, far + mine, total + other)[:2, :16]
    return (jnp.transpose(arranged, (0, 3, 1, 2)), mode_gram)


def solution(mesh):
    in_specs = (P("gx", None, "gy", "gz"), P("gy", None), P("gz", None), P())
    out_specs = (P("gy", "gz", "gx", None), P("gx", None))
    return jax.shard_map(
        on_device, mesh=mesh, in_specs=in_specs, out_specs=out_specs, check_vma=False
    )
```
